32 devices in a mesh: slab: 16 (over z, y, core), batch: 2 (over x).
Axes of the slice: x: 2, y: 2, z: 4, core: 2. Of those that a mesh axis runs over, the one named last changes fastest.
Arguments:
- features: float32 [2, 20, 64, 128, 128], P('batch', None, 'slab'), may hold values from -6 to 6
- cotangent: bfloat16 [2, 20, 64, 128, 128], P('batch', None, 'slab'), may hold values from -6 to 6
- spectral_weight: bfloat16 [768, 9600], P('slab'), may hold values from -6 to 6
- pointwise_weight: float32 [20, 20], replicated, may hold values from -1.25 to 1.25
Outputs:
- grad_features: bfloat16 [2, 20, 64, 128, 128], P('batch', None, 'slab')
- grad_spectral: float32 [768, 9600], P('slab')
The draws below stay inside these ranges and needn't reach their ends.
All inputs are finite; a program needn't handle non-finite values.
Results may differ from the reference program's by a relative error of at most 0.001.
Values sent between devices are 32-bit elements; how exact they have to be, the bound alone decides.
A program may use at most 128 MiB of HBM per device.

```python
import math
import jax
import jax.numpy as jnp
from jax import lax

C = 20
KX = 12
KY = 12
NY = 128
NX = 64
MZ = 64
MY = 768
SAMPLES = 2


def levels(rng, shape, pieces, smallest, largest):
    level = 1.0
    for position, blocks in pieces:
        draws = jax.random.uniform(jax.random.fold_in(jax.random.fold_in(rng, 6), position), (blocks,), jnp.float32, smallest / len(pieces), largest / len(pieces))
        level = level * jnp.repeat(jnp.exp(draws), shape[position] // blocks).reshape((-1,) + (1,) * (len(shape) - 1 - position))
    return level


def centred(rng, shape, spread, limit, cuts=(), kind=jnp.bfloat16):
    entries = jax.random.normal(rng, shape, jnp.float32) * spread
    if len(cuts) > 0:
        entries = levels(rng, shape, cuts, -0.22, 0.18) * entries
    return jnp.clip(entries, min=-limit, max=limit).astype(kind)


def setup_inputs(seed: int = 0) -> dict:
    splits = jax.random.split(jax.random.key(seed), 5)
    features = centred(splits[0], (SAMPLES, C, NX, NY, 2 * MZ), 1.0, 6.0, ((0, 2), (2, 16)), jnp.float32)
    cotangent = centred(splits[1], (SAMPLES, C, NX, NY, 2 * MZ), 1.0, 6.0, ((0, 2), (2, 16)))
    spectral_weight = centred(splits[2], (MY, KX * 2 * C * C), 1.0, 6.0, ((0, 16),))
    pointwise_weight = centred(splits[3], (C, C), C ** -0.5, 1.25, (), jnp.float32)
    return {"features": features, "cotangent": cotangent, "spectral_weight": spectral_weight, "pointwise_weight": pointwise_weight}


highest = lax.Precision.HIGHEST


def product(spec, left, right):
    return jnp.einsum(spec, left, right, precision=highest)


def signed(count):
    steps = jnp.arange(count, dtype=jnp.int32)
    return jnp.where(steps < count // 2, steps, steps - count)


def line_tables(count, length):
    phase = jnp.mod(signed(count)[:, None] * jnp.arange(length, dtype=jnp.int32)[None, :], length)
    angle = phase.astype(jnp.float32) * (2.0 * math.pi / length)
    return jnp.cos(angle), jnp.sin(angle)


def rotate_pair(spec, first_table, second_table, real_part, imag_part):
    out_real = product(spec, first_table, real_part) + product(spec, second_table, imag_part)
    out_imag = product(spec, first_table, imag_part) - product(spec, second_table, real_part)
    return out_real, out_imag


def spectra_lines(values, first_table, second_table):
    out_real, out_imag = rotate_pair("ay,scxyk->scxak", first_table, second_table, values[..., :MZ], values[..., MZ:])
    shape = out_real.shape[:3] + (out_real.shape[3] * MZ,)
    return jnp.stack([out_real.reshape(shape), out_imag.reshape(shape)], 3)


def lines_back(lines, first_table, second_table):
    shape = lines.shape[:3] + (KY, MZ)
    out_real, out_imag = rotate_pair("ya,scxak->scxyk", first_table, second_table, lines[:, :, :, 0].reshape(shape), lines[:, :, :, 1].reshape(shape))
    return jnp.concatenate([out_real, out_imag], axis=-1)


def to_owner(lines, first_table, second_table):
    out_real, out_imag = rotate_pair("ax,scxm->masc", first_table, second_table, lines[:, :, :, 0], lines[:, :, :, 1])
    return jnp.stack([out_real, out_imag], 2)


def from_owner(owner, first_table, second_table):
    out_real, out_imag = rotate_pair("xa,masc->scxm", first_table, second_table, owner[:, :, 0], owner[:, :, 1])
    return jnp.stack([out_real, out_imag], 3)


def mix_adjoint(grad_owner, weights):
    spec = "maso,maio->masi"
    out_real = product(spec, grad_owner[:, :, 0], weights[:, :, 0]) + product(spec, grad_owner[:, :, 1], weights[:, :, 1])
    out_imag = product(spec, grad_owner[:, :, 1], weights[:, :, 0]) - product(spec, grad_owner[:, :, 0], weights[:, :, 1])
    return jnp.stack([out_real, out_imag], 2)


def weight_terms(owner, grad_owner):
    spec = "masi,maso->maio"
    out_real = product(spec, owner[:, :, 0], grad_owner[:, :, 0]) + product(spec, owner[:, :, 1], grad_owner[:, :, 1])
    out_imag = product(spec, owner[:, :, 0], grad_owner[:, :, 1]) - product(spec, owner[:, :, 1], grad_owner[:, :, 0])
    return jnp.stack([out_real, out_imag], 2)


def reference(features, cotangent, spectral_weight, pointwise_weight):
    cos_y, sin_y = line_tables(KY, NY)
    cos_x, sin_x = line_tables(KX, NX)
    weights = spectral_weight.astype(jnp.float32).reshape(MY, KX, 2, C, C)

    def sample_step(total, inputs):
        sample = inputs[0][None]
        upstream = inputs[1].astype(jnp.float32)[None]
        lines = spectra_lines(sample, cos_y, sin_y)
        grad_lines = spectra_lines(upstream, cos_y, sin_y) / (NX * NY)
        both = to_owner(jnp.concatenate([lines, grad_lines], axis=0), cos_x, sin_x)
        owner = both[:, :, :, :1]
        grad_mixed = both[:, :, :, 1:]
        total = total + weight_terms(owner, grad_mixed)
        grad_back = from_owner(mix_adjoint(grad_mixed, weights), cos_x.T, -sin_x.T)
        grad_spatial = lines_back(grad_back, cos_y.T, -sin_y.T)
        grad_sample = grad_spatial + product("oc,soxyw->scxyw", pointwise_weight, upstream)
        return total, grad_sample[0].astype(jnp.bfloat16)

    start = jnp.zeros((MY, KX, 2, C, C), jnp.float32)
    total, grad_features = lax.scan(sample_step, start, (features, cotangent))
    return grad_features, total.reshape(MY, KX * 2 * C * C)
```

```python
import functools
import math

import jax
import jax.numpy as jnp
import numpy as np
from jax import lax
from jax.experimental import pallas as pl
from jax.experimental.pallas import tpu as pltpu
from jax.sharding import PartitionSpec as P

KX = 12
KY = 12
PAD = 16
HALF = KX // 2
TERMS = KX + 1
ROWS = 16

f32 = jnp.float32
bf16 = jnp.bfloat16


def angles(count, length):
    steps = np.arange(count)
    signed = np.where(steps < count // 2, steps, steps - count)
    turns = np.mod(signed[:, None] * np.arange(length)[None, :], length)
    return turns * (2.0 * math.pi / length)


def halves(value):
    high = value.astype(bf16)
    return high, (value - high.astype(f32)).astype(bf16)


def np_halves(value):
    value = np.asarray(value, np.float32)
    high = value.astype(jnp.bfloat16)
    return high, (value - high.astype(np.float32)).astype(jnp.bfloat16)


def padded(table, rows):
    return np.concatenate([table, np.zeros((rows - table.shape[0], table.shape[1]))], 0)


def forward_table(length):
    angle = angles(KY, length)
    both = np.concatenate([padded(np.cos(angle), PAD), padded(np.sin(angle), PAD)], 0)
    high, low = np_halves(both)
    top = np.concatenate([high, high], 1)
    bottom = np.concatenate([low, np.zeros_like(low)], 1)
    return np.concatenate([top, bottom], 0)


def backward_table(length):
    angle = angles(KY, length)
    both = np.concatenate([padded(np.cos(angle), PAD), padded(np.sin(angle), PAD)], 0).T
    high, low = np_halves(both)
    return np.concatenate([high, high, low], 1)


def plane_terms(length):
    turns = np.mod(np.arange(HALF + 1)[:, None] * np.arange(length)[None, :], length)
    angle = turns * (2.0 * math.pi / length)
    return np.concatenate([np.cos(angle), np.sin(angle)[1:]], 0).astype(np.float32).reshape(-1)


def spread_table(channels, width):
    table = np.zeros((2 * channels, 2 * width), np.float32)
    for c in range(channels):
        for o in range(channels):
            table[c, c * channels + o] = 1.0
            table[channels + o, width + c * channels + o] = 1.0
    return np.concatenate([table, table], 0).astype(jnp.bfloat16)


def collect_table(channels, rows, width):
    table = np.zeros((rows, width), np.float32)
    for c in range(channels):
        table[c, c * channels : (c + 1) * channels] = 1.0
    return table.astype(jnp.bfloat16)


def swap(value, owned):
    lane = lax.broadcasted_iota(jnp.int32, value.shape, 1)
    up = pltpu.roll(value, owned, 1)
    down = pltpu.roll(value, 128 - owned, 1)
    return jnp.where(lane < owned, down, jnp.where(lane < 2 * owned, -up, 0.0))


def pieces(owner, owned, depth):
    out = []
    mode = owner * owned
    while mode < (owner + 1) * owned:
        a, j = divmod(mode, depth)
        count = min(depth - j, (owner + 1) * owned - mode)
        out.append((mode - owner * owned, a, j, count))
        mode += count
    return out


def shifted(value, amount):
    amount %= 128
    return value if amount == 0 else pltpu.roll(value, amount, 1)


def kernel(
    n,
    peers,
    feat_ref,
    cot_ref,
    w_ref,
    kron_ref,
    fwd_ref,
    bwd_ref,
    spread_ref,
    collect_ref,
    plane_ref,
    gf_ref,
    gw_ref,
    lines,
    send,
    recv,
    spec,
    adj,
    send2,
    recv2,
    back,
    point,
    send_sem,
    recv_sem,
    send2_sem,
    recv2_sem,
    spec_send_sem,
    spec_recv_sem,
    local_sem,
):
    channels, planes, length, lanes = feat_ref.shape
    depth = lanes // 2
    owned = w_ref.shape[0]
    both = 2 * channels
    me = lax.axis_index("slab")
    mine = lax.axis_index("batch")
    scale = 1.0 / (planes * n * length)
    pair = 2

    barrier = pltpu.get_barrier_semaphore()

    def greet(step, carry):
        pl.semaphore_signal(
            barrier, inc=1, device_id=(lax.rem(me + step, n), mine), device_id_type=pl.DeviceIdType.MESH
        )
        return carry

    lax.fori_loop(1, n, greet, 0)

    def greet_batch(step, carry):
        pl.semaphore_signal(
            barrier, inc=1, device_id=(me, lax.rem(mine + step, peers)), device_id_type=pl.DeviceIdType.MESH
        )
        return carry

    lax.fori_loop(1, peers, greet_batch, 0)

    lane16 = lax.broadcasted_iota(jnp.int32, (PAD, lanes), 1)
    sign = jnp.where(lane16 < depth, 1.0, -1.0).astype(f32)

    def store_lines(out, row, first, c):
        total = out[: 2 * PAD] + out[2 * PAD :]
        for k in range(pair):
            part = total[:, k * lanes : (k + 1) * lanes]
            value = part[:PAD] + sign * pltpu.roll(part[PAD:], depth, 1)
            if row:
                value = value * scale
            lines[pl.ds((first + k) * both + row * channels + c, PAD, stride=planes * both), :] = value

    def along_y(c, carry):
        for first in range(0, planes, pair):
            block = jnp.concatenate([feat_ref[c, first + k] for k in range(pair)], 1)
            high, low = halves(block)
            out = jnp.dot(
                fwd_ref[...], jnp.concatenate([high, low], 0), preferred_element_type=f32
            )
            store_lines(out, 0, first, c)
            block = jnp.concatenate([cot_ref[c, first + k] for k in range(pair)], 1)
            out = jnp.dot(fwd_ref[:, :length], block, preferred_element_type=f32)
            store_lines(out, 1, first, c)
        return carry

    lax.fori_loop(0, channels, along_y, 0)

    lane8 = lax.broadcasted_iota(jnp.int32, (8, lanes), 1)
    groups = both // 8

    def fetch(x, owner, group):
        value = jnp.zeros((8, lanes), f32)
        for start, a, j, count in pieces(owner, owned, depth):
            row = pl.multiple_of((a * planes + x) * both + group * 8, 8)
            source = lines[pl.ds(row, 8), :]
            for part in range(2):
                at = part * owned + start
                moved = shifted(source, at - (part * depth + j))
                value = jnp.where((lane8 >= at) & (lane8 < at + count), moved, value)
        return value

    room = lanes - 2 * owned

    def pack(x, carry):
        for owner in range(n):
            extra = fetch(x, owner, groups - 1)
            for group in range(groups - 1):
                value = fetch(x, owner, group)
                if group < 3:
                    moved = shifted(extra, 2 * owned - group * room)
                    value = jnp.where(lane8 < 2 * owned, value, moved)
                send[owner, x, group * 8 : group * 8 + 8, :] = value
        return carry

    lax.fori_loop(0, planes, pack, 0)

    pl.semaphore_wait(barrier, n - 1 + peers - 1)

    def first_copy(step):
        other = lax.rem(me + step, n)
        return pltpu.make_async_remote_copy(
            src_ref=send.at[other],
            dst_ref=recv.at[me],
            send_sem=send_sem.at[step],
            recv_sem=recv_sem.at[step],
            device_id=(other, mine),
            device_id_type=pl.DeviceIdType.MESH,
        )

    def start_first(step, carry):
        first_copy(step).start()
        return carry

    lax.fori_loop(1, n, start_first, 0)
    local = pltpu.make_async_copy(send.at[me], recv.at[me], local_sem.at[0])
    local.start()

    tall = channels * ROWS

    def mix_cells(x, carry):
        for block in range(0, length, ROWS):
            value = cot_ref[:, x, block : block + ROWS, :].reshape(tall, lanes)
            out = jnp.dot(kron_ref[...], value, preferred_element_type=f32)
            total = out[:tall] + out[tall:]
            point[:, x, block : block + ROWS, :] = total.reshape(channels, ROWS, lanes)
        return carry

    lax.fori_loop(0, planes, mix_cells, 0)

    local.wait()

    def wait_first(step, carry):
        first_copy(step).wait()
        return carry

    lax.fori_loop(1, n, wait_first, 0)

    total_planes = n * planes
    tall_packed = both - 8
    sums = [[None] * 2 for _ in range(TERMS)]
    for part in range(2):
        rows = slice(part * 16, part * 16 + 16)

        def add_plane(x, carry, rows=rows):
            value = recv[x // planes, lax.rem(x, planes), rows, :]
            return tuple(
                carry[t] + plane_ref[t * total_planes + x] * value for t in range(TERMS)
            )

        got = lax.fori_loop(
            0, total_planes, add_plane, tuple(jnp.zeros((16, lanes), f32) for _ in range(TERMS)), unroll=4
        )
        for t in range(TERMS):
            sums[t][part] = got[t]

    lane_full = lax.broadcasted_iota(jnp.int32, (both, lanes), 1)

    def unpack(t):
        main = jnp.concatenate(sums[t], 0)
        last = jnp.zeros((8, lanes), f32)
        for group in range(3):
            moved = shifted(main[group * 8 : group * 8 + 8], group * room - 2 * owned)
            last = jnp.where((lane8 >= group * room) & (lane8 < (group + 1) * room), moved, last)
        whole = jnp.concatenate([main, last], 0)
        return jnp.where(lane_full < 2 * owned, whole, 0.0)

    for k in range(HALF + 1):
        even = unpack(k)
        if k == 0:
            spec[mine, 0] = even
            continue
        odd = swap(unpack(HALF + k), owned)
        if k < HALF:
            spec[mine, k] = even + odd
        spec[mine, KX - k] = even - odd

    def spec_copy(step):
        other = lax.rem(mine + step, peers)
        return pltpu.make_async_remote_copy(
            src_ref=spec.at[mine],
            dst_ref=spec.at[mine],
            send_sem=spec_send_sem.at[step],
            recv_sem=spec_recv_sem.at[step],
            device_id=(me, other),
            device_id_type=pl.DeviceIdType.MESH,
        )

    for step in range(1, peers):
        spec_copy(step).start()

    square = channels * channels
    width = spread_ref.shape[1] // 2

    def spread(sample, k):
        high, low = halves(jnp.concatenate([spec[sample, k]], 0).T)
        return jnp.dot(
            jnp.concatenate([high, low], 1), spread_ref[...], preferred_element_type=f32
        )

    for k in range(KX):
        wide = spread(mine, k)[:, width : width + square]
        real, imag = wide[:owned], wide[owned : 2 * owned]
        w_real = w_ref[:, k * 2 * square : (k * 2 + 1) * square].astype(f32)
        w_imag = w_ref[:, (k * 2 + 1) * square : (k * 2 + 2) * square].astype(f32)
        mixed = jnp.concatenate(
            [
                real * w_real + imag * w_imag,
                imag * w_real - real * w_imag,
                jnp.zeros((lanes - 2 * owned, square), f32),
            ],
            0,
        )
        out = None
        for part in halves(mixed):
            term = lax.dot_general(
                collect_ref[...], part, (((1,), (1,)), ((), ())), preferred_element_type=f32
            )
            out = term if out is None else out + term
        adj[k] = out

    lane_half = lax.broadcasted_iota(jnp.int32, (16, lanes), 1)
    row_half = lax.broadcasted_iota(jnp.int32, (16, lanes), 0)

    def pack_back(value):
        main = value[:16]
        last = jnp.concatenate([value[16:24], jnp.zeros((8, lanes), f32)], 0)
        for group in range(3):
            moved = shifted(last, 2 * owned - group * room)
            if group:
                moved = pltpu.roll(moved, 4 * group, 0)
            here = (lane_half >= 2 * owned) & (row_half >= 4 * group) & (row_half < 4 * group + 4)
            main = jnp.where(here, moved, main)
        return main

    terms = [pack_back(adj[0])]
    for k in range(1, HALF):
        terms.append(pack_back(adj[k] + adj[KX - k]))
    terms.append(pack_back(adj[HALF]))
    for k in range(1, HALF):
        terms.append(pack_back(swap(adj[KX - k] - adj[k], owned)))
    terms.append(pack_back(swap(adj[HALF], owned)))

    def put_plane(x, carry):
        value = plane_ref[x] * carry[0]
        for t in range(1, TERMS):
            value = value + plane_ref[t * total_planes + x] * carry[t]
        send2[x // planes, lax.rem(x, planes)] = value
        return carry

    lax.fori_loop(0, total_planes, put_plane, tuple(terms), unroll=4)

    def second_copy(step):
        other = lax.rem(me + step, n)
        return pltpu.make_async_remote_copy(
            src_ref=send2.at[other],
            dst_ref=recv2.at[me],
            send_sem=send2_sem.at[step],
            recv_sem=recv2_sem.at[step],
            device_id=(other, mine),
            device_id_type=pl.DeviceIdType.MESH,
        )

    def start_second(step, carry):
        second_copy(step).start()
        return carry

    lax.fori_loop(1, n, start_second, 0)
    local2 = pltpu.make_async_copy(send2.at[me], recv2.at[me], local_sem.at[1])
    local2.start()

    for step in range(1, peers):
        spec_copy(step).wait()

    for k in range(KX):
        out_real = out_imag = None
        for sample in range(peers):
            wide = spread(sample, k)
            s_real, s_imag = wide[:owned, :square], wide[owned : 2 * owned, :square]
            g_real = wide[:owned, width : width + square]
            g_imag = wide[owned : 2 * owned, width : width + square]
            t_real = s_real * g_real + s_imag * g_imag
            t_imag = s_real * g_imag - s_imag * g_real
            out_real = t_real if out_real is None else out_real + t_real
            out_imag = t_imag if out_imag is None else out_imag + t_imag
        gw_ref[:, k * 2 * square : (k * 2 + 1) * square] = out_real
        gw_ref[:, (k * 2 + 1) * square : (k * 2 + 2) * square] = out_imag

    local2.wait()

    def wait_second(step, carry):
        second_copy(step).wait()
        return carry

    lax.fori_loop(1, n, wait_second, 0)

    tail = 24

    def unpack_back(x, carry):
        wholes = {}
        for owner in range(n):
            main = recv2[owner, x]
            last = jnp.zeros((16, lanes), f32)
            for group in range(3):
                moved = shifted(main, group * room - 2 * owned)
                if group:
                    moved = pltpu.roll(moved, 16 - 4 * group, 0)
                here = (lane_half >= group * room) & (lane_half < (group + 1) * room)
                last = jnp.where(here, moved, last)
            wholes[owner] = (main[:8], main[8:16], last[:8])
            for a in range(KY):
                first = a * depth // owned
                final = ((a + 1) * depth - 1) // owned
                if final != owner:
                    continue
                for group in range(3):
                    value = jnp.zeros((8, lanes), f32)
                    for source in range(first, final + 1):
                        for start, row, j, count in pieces(source, owned, depth):
                            if row != a:
                                continue
                            for part in range(2):
                                at = part * depth + j
                                moved = shifted(wholes[source][group], at - (part * owned + start))
                                value = jnp.where(
                                    (lane8 >= at) & (lane8 < at + count), moved, value
                                )
                    place = pl.multiple_of((a * planes + x) * tail + group * 8, 8)
                    back[pl.ds(place, 8), :] = value
        for a in range(KY, PAD):
            for group in range(3):
                place = pl.multiple_of((a * planes + x) * tail + group * 8, 8)
                back[pl.ds(place, 8), :] = jnp.zeros((8, lanes), f32)
        return carry

    lax.fori_loop(0, planes, unpack_back, 0)

    def finish(c, carry):
        for first in range(0, planes, pair):
            blocks = []
            for k in range(pair):
                value = back[pl.ds((first + k) * tail + c, PAD, stride=planes * tail), :]
                turned = -sign * pltpu.roll(value, depth, 1)
                blocks.append(jnp.concatenate([value, turned], 0))
            high, low = halves(jnp.concatenate(blocks, 1))
            out = jnp.dot(
                bwd_ref[...], jnp.concatenate([high, low, high], 0), preferred_element_type=f32
            )
            for k in range(pair):
                gf_ref[c, first + k] = (
                    point[c, first + k] + out[:, k * lanes : (k + 1) * lanes]
                ).astype(bf16)
        return carry

    lax.fori_loop(0, channels, finish, 0)


def shards(features, cotangent, spectral_weight, pointwise_weight):
    _, channels, planes, length, lanes = features.shape
    owned = spectral_weight.shape[0]
    n = lax.axis_size("slab")
    peers = lax.axis_size("batch")
    both = 2 * channels
    square = channels * channels
    width = -(-square // 128) * 128
    high = lax.reduce_precision(pointwise_weight.T, 8, 7)
    parts = jnp.concatenate([high, pointwise_weight.T - high], 0)
    kron = jnp.kron(parts, jnp.eye(ROWS, dtype=f32)).astype(bf16)
    vmem = pl.BlockSpec(memory_space=pltpu.VMEM)
    grad_features, grad_spectral = pl.pallas_call(
        functools.partial(kernel, n, peers),
        out_shape=(
            jax.ShapeDtypeStruct(features.shape[1:], bf16),
            jax.ShapeDtypeStruct(spectral_weight.shape, f32),
        ),
        in_specs=[vmem] * 8 + [pl.BlockSpec(memory_space=pltpu.SMEM)],
        out_specs=(vmem, vmem),
        scratch_shapes=[
            pltpu.VMEM((PAD * planes * both, lanes), f32),
            pltpu.VMEM((n, planes, both - 8, lanes), f32),
            pltpu.VMEM((n, planes, both - 8, lanes), f32),
            pltpu.VMEM((peers, KX, both, lanes), f32),
            pltpu.VMEM((KX, 24, lanes), f32),
            pltpu.VMEM((n, planes, 16, lanes), f32),
            pltpu.VMEM((n, planes, 16, lanes), f32),
            pltpu.VMEM((PAD * planes * 24, lanes), f32),
            pltpu.VMEM((channels, planes, length, lanes), f32),
            pltpu.SemaphoreType.DMA((n,)),
            pltpu.SemaphoreType.DMA((n,)),
            pltpu.SemaphoreType.DMA((n,)),
            pltpu.SemaphoreType.DMA((n,)),
            pltpu.SemaphoreType.DMA((peers,)),
            pltpu.SemaphoreType.DMA((peers,)),
            pltpu.SemaphoreType.DMA((2,)),
        ],
        compiler_params=pltpu.CompilerParams(
            collective_id=0, has_side_effects=True, vmem_limit_bytes=58 * 1024 * 1024
        ),
    )(
        features[0],
        cotangent[0],
        spectral_weight,
        kron,
        jnp.asarray(forward_table(length)),
        jnp.asarray(backward_table(length)),
        jnp.asarray(spread_table(channels, width)),
        jnp.asarray(collect_table(channels, 24, square)),
        jnp.asarray(plane_terms(planes * n)),
    )
    return grad_features[None], grad_spectral


def solution(mesh):
    placed = (
        P("batch", None, "slab", None, None),
        P("batch", None, "slab", None, None),
        P("slab", None),
        P(),
    )
    return jax.shard_map(
        shards,
        mesh=mesh,
        in_specs=placed,
        out_specs=(P("batch", None, "slab", None, None), P("slab", None)),
        check_vma=False,
    )
```

```python
import functools
import math

import jax
import jax.numpy as jnp
import numpy as np
from jax import lax
from jax.experimental import pallas as pl
from jax.experimental.pallas import tpu as pltpu
from jax.sharding import PartitionSpec as P

KX = 12
KY = 12
PAD = 16
HALF = KX // 2
TERMS = KX + 1
ROWS = 16

f32 = jnp.float32
bf16 = jnp.bfloat16


def angles(count, length):
    steps = np.arange(count)
    signed = np.where(steps < count // 2, steps, steps - count)
    turns = np.mod(signed[:, None] * np.arange(length)[None, :], length)
    return turns * (2.0 * math.pi / length)


def halves(value):
    high = value.astype(bf16)
    return high, (value - high.astype(f32)).astype(bf16)


def np_halves(value):
    value = np.asarray(value, np.float32)
    high = value.astype(jnp.bfloat16)
    return high, (value - high.astype(np.float32)).astype(jnp.bfloat16)


def padded(table, rows):
    return np.concatenate([table, np.zeros((rows - table.shape[0], table.shape[1]))], 0)


def forward_table(length):
    angle = angles(KY, length)
    both = np.concatenate([padded(np.cos(angle), PAD), padded(np.sin(angle), PAD)], 0)
    high, low = np_halves(both)
    top = np.concatenate([high, high], 1)
    bottom = np.concatenate([low, np.zeros_like(low)], 1)
    return np.concatenate([top, bottom], 0)


def backward_table(length):
    angle = angles(KY, length)
    both = np.concatenate([padded(np.cos(angle), PAD), padded(np.sin(angle), PAD)], 0).T
    high, low = np_halves(both)
    return np.concatenate([high, high, low], 1)


def plane_terms(length):
    turns = np.mod(np.arange(HALF + 1)[:, None] * np.arange(length)[None, :], length)
    angle = turns * (2.0 * math.pi / length)
    return np.concatenate([np.cos(angle), np.sin(angle)[1:]], 0).astype(np.float32).reshape(-1)


def spread_tables(channels, rows, width):
    tables = np.zeros((2, rows, width), np.float32)
    for c in range(channels):
        for o in range(channels):
            tables[0, c, c * channels + o] = 1.0
            tables[1, o, c * channels + o] = 1.0
    return np.concatenate([tables, tables], 1).astype(jnp.bfloat16)


def collect_table(channels, rows, width):
    table = np.zeros((rows, width), np.float32)
    for c in range(channels):
        table[c, c * channels : (c + 1) * channels] = 1.0
    return table.astype(jnp.bfloat16)


def swap(value, owned):
    lane = lax.broadcasted_iota(jnp.int32, value.shape, 1)
    up = pltpu.roll(value, owned, 1)
    down = pltpu.roll(value, 128 - owned, 1)
    return jnp.where(lane < owned, down, jnp.where(lane < 2 * owned, -up, 0.0))


def pieces(owner, owned, depth):
    out = []
    mode = owner * owned
    while mode < (owner + 1) * owned:
        a, j = divmod(mode, depth)
        count = min(depth - j, (owner + 1) * owned - mode)
        out.append((mode - owner * owned, a, j, count))
        mode += count
    return out


def shifted(value, amount):
    amount %= 128
    return value if amount == 0 else pltpu.roll(value, amount, 1)


def kernel(
    n,
    peers,
    feat_ref,
    cot_ref,
    w_ref,
    pw_ref,
    expand_ref,
    fwd_ref,
    bwd_ref,
    spread_ref,
    collect_ref,
    plane_ref,
    gf_ref,
    gw_ref,
    lines,
    send,
    recv,
    spec,
    adj,
    send2,
    recv2,
    back,
    point,
    kron_ref,
    send_sem,
    recv_sem,
    send2_sem,
    recv2_sem,
    spec_send_sem,
    spec_recv_sem,
    local_sem,
):
    channels, planes, length, lanes = feat_ref.shape
    depth = lanes // 2
    owned = w_ref.shape[0]
    tail = 24
    me = lax.axis_index("slab")
    mine = lax.axis_index("batch")
    scale = 1.0 / (planes * n * length)
    pair = 2

    barrier = pltpu.get_barrier_semaphore()

    def greet(step, carry):
        pl.semaphore_signal(
            barrier, inc=1, device_id=(lax.rem(me + step, n), mine), device_id_type=pl.DeviceIdType.MESH
        )
        return carry

    lax.fori_loop(1, n, greet, 0)

    def greet_batch(step, carry):
        pl.semaphore_signal(
            barrier, inc=1, device_id=(me, lax.rem(mine + step, peers)), device_id_type=pl.DeviceIdType.MESH
        )
        return carry

    lax.fori_loop(1, peers, greet_batch, 0)

    lane16 = lax.broadcasted_iota(jnp.int32, (PAD, lanes), 1)
    sign = jnp.where(lane16 < depth, 1.0, -1.0).astype(f32)

    def store_lines(out, kind, first, c):
        total = out[: 2 * PAD] + out[2 * PAD :]
        for k in range(pair):
            part = total[:, k * lanes : (k + 1) * lanes]
            value = part[:PAD] + sign * pltpu.roll(part[PAD:], depth, 1)
            if kind:
                value = value * scale
            lines[kind, pl.ds((first + k) * tail + c, PAD, stride=planes * tail), :] = value

    def field_lines(c, carry):
        for first in range(0, planes, pair):
            block = jnp.concatenate([feat_ref[c, first + k] for k in range(pair)], 1)
            high, low = halves(block)
            out = jnp.dot(
                fwd_ref[...], jnp.concatenate([high, low], 0), preferred_element_type=f32
            )
            store_lines(out, 0, first, c)
        return carry

    def gradient_lines(c, carry):
        for first in range(0, planes, pair):
            block = jnp.concatenate([cot_ref[c, first + k] for k in range(pair)], 1)
            out = jnp.dot(fwd_ref[:, :length], block, preferred_element_type=f32)
            store_lines(out, 1, first, c)
        return carry

    lane8 = lax.broadcasted_iota(jnp.int32, (8, lanes), 1)
    row8 = lax.broadcasted_iota(jnp.int32, (8, lanes), 0)
    lane_half = lax.broadcasted_iota(jnp.int32, (16, lanes), 1)
    row_half = lax.broadcasted_iota(jnp.int32, (16, lanes), 0)
    room = lanes - 2 * owned

    def fold(main, last):
        last = jnp.concatenate([last, jnp.zeros((8, lanes), f32)], 0)
        for group in range(3):
            moved = shifted(last, 2 * owned - group * room)
            if group:
                moved = pltpu.roll(moved, 4 * group, 0)
            here = (lane_half >= 2 * owned) & (row_half >= 4 * group) & (row_half < 4 * group + 4)
            main = jnp.where(here, moved, main)
        return main

    def unfold(main):
        last = jnp.zeros((16, lanes), f32)
        for group in range(3):
            moved = shifted(main, group * room - 2 * owned)
            if group:
                moved = pltpu.roll(moved, 16 - 4 * group, 0)
            here = (lane_half >= group * room) & (lane_half < (group + 1) * room)
            last = jnp.where(here, moved, last)
        return jnp.where(row8 < 4, last[:8], 0.0)

    def pack_kind(kind):
        def pack(x, carry):
            for owner in range(n):
                values = []
                for group in range(3):
                    value = jnp.zeros((8, lanes), f32)
                    for start, a, j, count in pieces(owner, owned, depth):
                        row = pl.multiple_of((a * planes + x) * tail + group * 8, 8)
                        source = lines[kind, pl.ds(row, 8), :]
                        for part in range(2):
                            at = part * owned + start
                            moved = shifted(source, at - (part * depth + j))
                            value = jnp.where((lane8 >= at) & (lane8 < at + count), moved, value)
                    values.append(value)
                send[kind, owner, x] = fold(jnp.concatenate(values[:2], 0), values[2])
            return carry

        lax.fori_loop(0, planes, pack, 0)

    def first_copy(kind, step):
        other = lax.rem(me + step, n)
        return pltpu.make_async_remote_copy(
            src_ref=send.at[kind, other],
            dst_ref=recv.at[kind, me],
            send_sem=send_sem.at[kind, step],
            recv_sem=recv_sem.at[kind, step],
            device_id=(other, mine),
            device_id_type=pl.DeviceIdType.MESH,
        )

    def own_copy(kind):
        return pltpu.make_async_copy(send.at[kind, me], recv.at[kind, me], local_sem.at[kind])

    def start_first(kind):
        def start(step, carry):
            first_copy(kind, step).start()
            return carry

        lax.fori_loop(1, n, start, 0)
        own_copy(kind).start()

    def wait_first(kind):
        def wait(step, carry):
            first_copy(kind, step).wait()
            return carry

        own_copy(kind).wait()
        lax.fori_loop(1, n, wait, 0)

    lax.fori_loop(0, channels, gradient_lines, 0)
    pack_kind(1)
    pl.semaphore_wait(barrier, n - 1 + peers - 1)
    start_first(1)
    lax.fori_loop(0, channels, field_lines, 0)
    pack_kind(0)
    start_first(0)

    tall = channels * ROWS
    same = (
        lax.broadcasted_iota(jnp.int32, (tall, tall), 0)
        ^ lax.broadcasted_iota(jnp.int32, (tall, tall), 1)
    ) & (ROWS - 1)
    across = (((1,), (1,)), ((), ()))
    for place, part in enumerate(halves(pw_ref[...])):
        outer = lax.dot_general(expand_ref[...], part, across, preferred_element_type=f32)
        inner = lax.dot_general(
            outer.astype(bf16), expand_ref[...], across, preferred_element_type=f32
        )
        kron_ref[place * tall : (place + 1) * tall, :] = jnp.where(same == 0, inner, 0.0).astype(bf16)

    def mix_cells(x, carry):
        for block in range(0, length, ROWS):
            value = cot_ref[:, x, block : block + ROWS, :].reshape(tall, lanes)
            out = jnp.dot(kron_ref[...], value, preferred_element_type=f32)
            total = out[:tall] + out[tall:]
            point[:, x, block : block + ROWS, :] = total.reshape(channels, ROWS, lanes)
        return carry

    lax.fori_loop(0, planes, mix_cells, 0)

    total_planes = n * planes

    def spec_copy(kind, step):
        other = lax.rem(mine + step, peers)
        return pltpu.make_async_remote_copy(
            src_ref=spec.at[mine, kind],
            dst_ref=spec.at[mine, kind],
            send_sem=spec_send_sem.at[kind, step],
            recv_sem=spec_recv_sem.at[kind, step],
            device_id=(me, other),
            device_id_type=pl.DeviceIdType.MESH,
        )

    def along_x(kind):
        def add_plane(x, carry):
            value = recv[kind, x // planes, lax.rem(x, planes)]
            return tuple(
                carry[t] + plane_ref[t * total_planes + x] * value for t in range(TERMS)
            )

        zero = jnp.zeros((16, lanes), f32)
        sums = lax.fori_loop(0, total_planes, add_plane, (zero,) * TERMS, unroll=4)

        def unpack(t):
            main = jnp.where(lane_half < 2 * owned, sums[t], 0.0)
            return jnp.concatenate([main, unfold(sums[t])], 0)

        for k in range(HALF + 1):
            even = unpack(k)
            if k == 0:
                spec[mine, kind, 0] = even
                continue
            odd = swap(unpack(HALF + k), owned)
            if k < HALF:
                spec[mine, kind, k] = even + odd
            spec[mine, kind, KX - k] = even - odd
        for step in range(1, peers):
            spec_copy(kind, step).start()

    wait_first(1)
    along_x(1)

    square = channels * channels

    def spread(sample, kind, k):
        high, low = halves(spec[sample, kind, k].T)
        return jnp.dot(
            jnp.concatenate([high, low], 1), spread_ref[kind], preferred_element_type=f32
        )[:, :square]

    for k in range(KX):
        wide = spread(mine, 1, k)
        real, imag = wide[:owned], wide[owned : 2 * owned]
        w_real = w_ref[:, k * 2 * square : (k * 2 + 1) * square].astype(f32)
        w_imag = w_ref[:, (k * 2 + 1) * square : (k * 2 + 2) * square].astype(f32)
        mixed = jnp.concatenate(
            [
                real * w_real + imag * w_imag,
                imag * w_real - real * w_imag,
                jnp.zeros((lanes - 2 * owned, square), f32),
            ],
            0,
        )
        out = None
        for part in halves(mixed):
            term = lax.dot_general(
                collect_ref[...], part, (((1,), (1,)), ((), ())), preferred_element_type=f32
            )
            out = term if out is None else out + term
        adj[k] = out

    def pack_back(value):
        return fold(value[:16], value[16:])

    terms = [pack_back(adj[0])]
    for k in range(1, HALF):
        terms.append(pack_back(adj[k] + adj[KX - k]))
    terms.append(pack_back(adj[HALF]))
    for k in range(1, HALF):
        terms.append(pack_back(swap(adj[KX - k] - adj[k], owned)))
    terms.append(pack_back(swap(adj[HALF], owned)))

    def put_plane(x, carry):
        value = plane_ref[x] * carry[0]
        for t in range(1, TERMS):
            value = value + plane_ref[t * total_planes + x] * carry[t]
        send2[x // planes, lax.rem(x, planes)] = value
        return carry

    lax.fori_loop(0, total_planes, put_plane, tuple(terms), unroll=4)

    def second_copy(step):
        other = lax.rem(me + step, n)
        return pltpu.make_async_remote_copy(
            src_ref=send2.at[other],
            dst_ref=recv2.at[me],
            send_sem=send2_sem.at[step],
            recv_sem=recv2_sem.at[step],
            device_id=(other, mine),
            device_id_type=pl.DeviceIdType.MESH,
        )

    def start_second(step, carry):
        second_copy(step).start()
        return carry

    lax.fori_loop(1, n, start_second, 0)
    local2 = pltpu.make_async_copy(send2.at[me], recv2.at[me], local_sem.at[2])
    local2.start()

    wait_first(0)
    along_x(0)
    for kind in range(2):
        for step in range(1, peers):
            spec_copy(kind, step).wait()

    for k in range(KX):
        out_real = out_imag = None
        for sample in range(peers):
            wide, g_wide = spread(sample, 0, k), spread(sample, 1, k)
            s_real, s_imag = wide[:owned], wide[owned : 2 * owned]
            g_real, g_imag = g_wide[:owned], g_wide[owned : 2 * owned]
            t_real = s_real * g_real + s_imag * g_imag
            t_imag = s_real * g_imag - s_imag * g_real
            out_real = t_real if out_real is None else out_real + t_real
            out_imag = t_imag if out_imag is None else out_imag + t_imag
        gw_ref[:, k * 2 * square : (k * 2 + 1) * square] = out_real
        gw_ref[:, (k * 2 + 1) * square : (k * 2 + 2) * square] = out_imag

    local2.wait()

    def wait_second(step, carry):
        second_copy(step).wait()
        return carry

    lax.fori_loop(1, n, wait_second, 0)

    def unpack_back(x, carry):
        wholes = {}
        for owner in range(n):
            main = recv2[owner, x]
            wholes[owner] = (main[:8], main[8:16], unfold(main))
            for a in range(KY):
                first = a * depth // owned
                final = ((a + 1) * depth - 1) // owned
                if final != owner:
                    continue
                for group in range(3):
                    value = jnp.zeros((8, lanes), f32)
                    for source in range(first, final + 1):
                        for start, row, j, count in pieces(source, owned, depth):
                            if row != a:
                                continue
                            for part in range(2):
                                at = part * depth + j
                                moved = shifted(wholes[source][group], at - (part * owned + start))
                                value = jnp.where(
                                    (lane8 >= at) & (lane8 < at + count), moved, value
                                )
                    place = pl.multiple_of((a * planes + x) * tail + group * 8, 8)
                    back[pl.ds(place, 8), :] = value
        for a in range(KY, PAD):
            for group in range(3):
                place = pl.multiple_of((a * planes + x) * tail + group * 8, 8)
                back[pl.ds(place, 8), :] = jnp.zeros((8, lanes), f32)
        return carry

    lax.fori_loop(0, planes, unpack_back, 0)

    def finish(c, carry):
        for first in range(0, planes, pair):
            blocks = []
            for k in range(pair):
                value = back[pl.ds((first + k) * tail + c, PAD, stride=planes * tail), :]
                turned = -sign * pltpu.roll(value, depth, 1)
                blocks.append(jnp.concatenate([value, turned], 0))
            high, low = halves(jnp.concatenate(blocks, 1))
            out = jnp.dot(
                bwd_ref[...], jnp.concatenate([high, low, high], 0), preferred_element_type=f32
            )
            for k in range(pair):
                gf_ref[c, first + k] = (
                    point[c, first + k] + out[:, k * lanes : (k + 1) * lanes]
                ).astype(bf16)
        return carry

    lax.fori_loop(0, channels, finish, 0)


def shards(features, cotangent, spectral_weight, pointwise_weight):
    _, channels, planes, length, lanes = features.shape
    owned = spectral_weight.shape[0]
    n = lax.axis_size("slab")
    peers = lax.axis_size("batch")
    tail = 24
    square = channels * channels
    width = -(-square // 128) * 128
    vmem = pl.BlockSpec(memory_space=pltpu.VMEM)
    grad_features, grad_spectral = pl.pallas_call(
        functools.partial(kernel, n, peers),
        out_shape=(
            jax.ShapeDtypeStruct(features.shape[1:], bf16),
            jax.ShapeDtypeStruct(spectral_weight.shape, f32),
        ),
        in_specs=[vmem] * 9 + [pl.BlockSpec(memory_space=pltpu.SMEM)],
        out_specs=(vmem, vmem),
        scratch_shapes=[
            pltpu.VMEM((2, PAD * planes * tail, lanes), f32),
            pltpu.VMEM((2, n, planes, 16, lanes), f32),
            pltpu.VMEM((2, n, planes, 16, lanes), f32),
            pltpu.VMEM((peers, 2, KX, tail, lanes), f32),
            pltpu.VMEM((KX, 24, lanes), f32),
            pltpu.VMEM((n, planes, 16, lanes), f32),
            pltpu.VMEM((n, planes, 16, lanes), f32),
            pltpu.VMEM((PAD * planes * 24, lanes), f32),
            pltpu.VMEM((channels, planes, length, lanes), f32),
            pltpu.VMEM((2 * channels * ROWS, channels * ROWS), bf16),
            pltpu.SemaphoreType.DMA((2, n)),
            pltpu.SemaphoreType.DMA((2, n)),
            pltpu.SemaphoreType.DMA((n,)),
            pltpu.SemaphoreType.DMA((n,)),
            pltpu.SemaphoreType.DMA((2, peers)),
            pltpu.SemaphoreType.DMA((2, peers)),
            pltpu.SemaphoreType.DMA((3,)),
        ],
        compiler_params=pltpu.CompilerParams(
            collective_id=0, has_side_effects=True, vmem_limit_bytes=58 * 1024 * 1024
        ),
    )(
        features[0],
        cotangent[0],
        spectral_weight,
        pointwise_weight,
        jnp.asarray(np.repeat(np.eye(channels), ROWS, 0).astype(jnp.bfloat16)),
        jnp.asarray(forward_table(length)),
        jnp.asarray(backward_table(length)),
        jnp.asarray(spread_tables(channels, tail, width)),
        jnp.asarray(collect_table(channels, 24, square)),
        jnp.asarray(plane_terms(planes * n)),
    )
    return grad_features[None], grad_spectral


def solution(mesh):
    placed = (
        P("batch", None, "slab", None, None),
        P("batch", None, "slab", None, None),
        P("slab", None),
        P(),
    )
    return jax.shard_map(
        shards,
        mesh=mesh,
        in_specs=placed,
        out_specs=(P("batch", None, "slab", None, None), P("slab", None)),
        check_vma=False,
    )
```

```python
import functools
import math

import jax
import jax.numpy as jnp
import numpy as np
from jax import lax
from jax.experimental import pallas as pl
from jax.experimental.pallas import tpu as pltpu
from jax.sharding import PartitionSpec as P

KX = 12
KY = 12
PAD = 16
HALF = KX // 2
TERMS = KX + 1
ROWS = 16

f32 = jnp.float32
bf16 = jnp.bfloat16


def angles(count, length):
    steps = np.arange(count)
    signed = np.where(steps < count // 2, steps, steps - count)
    turns = np.mod(signed[:, None] * np.arange(length)[None, :], length)
    return turns * (2.0 * math.pi / length)


def halves(value):
    high = value.astype(bf16)
    return high, (value - high.astype(f32)).astype(bf16)


def np_halves(value):
    value = np.asarray(value, np.float32)
    high = value.astype(jnp.bfloat16)
    return high, (value - high.astype(np.float32)).astype(jnp.bfloat16)


def padded(table, rows):
    return np.concatenate([table, np.zeros((rows - table.shape[0], table.shape[1]))], 0)


def forward_table(length):
    angle = angles(KY, length)
    both = np.concatenate([padded(np.cos(angle), PAD), padded(np.sin(angle), PAD)], 0)
    high, low = np_halves(both)
    top = np.concatenate([high, high], 1)
    bottom = np.concatenate([low, np.zeros_like(low)], 1)
    return np.concatenate([top, bottom], 0)


def backward_table(length):
    angle = angles(KY, length)
    both = np.concatenate([padded(np.cos(angle), PAD), padded(np.sin(angle), PAD)], 0).T
    high, low = np_halves(both)
    return np.concatenate([high, high, low], 1)


def plane_terms(length):
    turns = np.mod(np.arange(HALF + 1)[:, None] * np.arange(length)[None, :], length)
    angle = turns * (2.0 * math.pi / length)
    return np.concatenate([np.cos(angle), np.sin(angle)[1:]], 0).astype(np.float32).reshape(-1)


def spread_tables(channels, rows, width):
    tables = np.zeros((2, rows, width), np.float32)
    for c in range(channels):
        for o in range(channels):
            tables[0, c, c * channels + o] = 1.0
            tables[1, o, c * channels + o] = 1.0
    return np.concatenate([tables, tables], 1).astype(jnp.bfloat16)


def collect_table(channels, rows, width):
    table = np.zeros((rows, width), np.float32)
    for c in range(channels):
        table[c, c * channels : (c + 1) * channels] = 1.0
    return table.astype(jnp.bfloat16)


def swap(value, owned):
    lane = lax.broadcasted_iota(jnp.int32, value.shape, 1)
    up = pltpu.roll(value, owned, 1)
    down = pltpu.roll(value, 128 - owned, 1)
    return jnp.where(lane < owned, down, jnp.where(lane < 2 * owned, -up, 0.0))


def pieces(owner, owned, depth):
    out = []
    mode = owner * owned
    while mode < (owner + 1) * owned:
        a, j = divmod(mode, depth)
        count = min(depth - j, (owner + 1) * owned - mode)
        out.append((mode - owner * owned, a, j, count))
        mode += count
    return out


def shifted(value, amount):
    amount %= 128
    return value if amount == 0 else pltpu.roll(value, amount, 1)


def kernel(
    n,
    peers,
    feat_hbm,
    cot_hbm,
    w_hbm,
    pw_ref,
    expand_ref,
    fwd_ref,
    bwd_ref,
    spread_ref,
    collect_ref,
    plane_ref,
    gf_hbm,
    gw_hbm,
    feat_ref,
    cot_ref,
    w_ref,
    gf_ref,
    gw_ref,
    lines,
    send,
    recv,
    spec,
    adj,
    send2,
    recv2,
    back,
    point,
    kron_ref,
    send_sem,
    recv_sem,
    send2_sem,
    recv2_sem,
    spec_send_sem,
    spec_recv_sem,
    local_sem,
    cot_sem,
    feat_sem,
    w_sem,
    gf_sem,
    gw_sem,
):
    channels, planes, length, lanes = feat_ref.shape
    depth = lanes // 2
    owned = w_ref.shape[0]
    tail = 24
    me = lax.axis_index("slab")
    mine = lax.axis_index("batch")
    scale = 1.0 / (planes * n * length)
    pair = 2

    chunks = cot_sem.shape[0]
    per = channels // chunks

    def load(source, target, sem, chunk):
        at = pl.ds(chunk * per, per)
        return pltpu.make_async_copy(source.at[at], target.at[at], sem.at[chunk])

    for chunk in range(chunks):
        load(cot_hbm, cot_ref, cot_sem, chunk).start()
    barrier = pltpu.get_barrier_semaphore()

    def greet(step, carry):
        pl.semaphore_signal(
            barrier, inc=1, device_id=(lax.rem(me + step, n), mine), device_id_type=pl.DeviceIdType.MESH
        )
        return carry

    lax.fori_loop(1, n, greet, 0)

    def greet_batch(step, carry):
        pl.semaphore_signal(
            barrier, inc=1, device_id=(me, lax.rem(mine + step, peers)), device_id_type=pl.DeviceIdType.MESH
        )
        return carry

    lax.fori_loop(1, peers, greet_batch, 0)

    lane16 = lax.broadcasted_iota(jnp.int32, (PAD, lanes), 1)
    sign = jnp.where(lane16 < depth, 1.0, -1.0).astype(f32)

    def store_lines(out, kind, first, c):
        total = out[: 2 * PAD] + out[2 * PAD :]
        for k in range(pair):
            part = total[:, k * lanes : (k + 1) * lanes]
            value = part[:PAD] + sign * pltpu.roll(part[PAD:], depth, 1)
            if kind:
                value = value * scale
            lines[kind, pl.ds((first + k) * tail + c, PAD, stride=planes * tail), :] = value

    def field_lines(c, carry):
        for first in range(0, planes, pair):
            block = jnp.concatenate([feat_ref[c, first + k] for k in range(pair)], 1)
            high, low = halves(block)
            out = jnp.dot(
                fwd_ref[...], jnp.concatenate([high, low], 0), preferred_element_type=f32
            )
            store_lines(out, 0, first, c)
        return carry

    def gradient_lines(c, carry):
        for first in range(0, planes, pair):
            block = jnp.concatenate([cot_ref[c, first + k] for k in range(pair)], 1)
            out = jnp.dot(fwd_ref[:, :length], block, preferred_element_type=f32)
            store_lines(out, 1, first, c)
        return carry

    lane8 = lax.broadcasted_iota(jnp.int32, (8, lanes), 1)
    row8 = lax.broadcasted_iota(jnp.int32, (8, lanes), 0)
    lane_half = lax.broadcasted_iota(jnp.int32, (16, lanes), 1)
    row_half = lax.broadcasted_iota(jnp.int32, (16, lanes), 0)
    room = lanes - 2 * owned

    def fold(main, last):
        last = jnp.concatenate([last, jnp.zeros((8, lanes), f32)], 0)
        for group in range(3):
            moved = shifted(last, 2 * owned - group * room)
            if group:
                moved = pltpu.roll(moved, 4 * group, 0)
            here = (lane_half >= 2 * owned) & (row_half >= 4 * group) & (row_half < 4 * group + 4)
            main = jnp.where(here, moved, main)
        return main

    def unfold(main):
        last = jnp.zeros((16, lanes), f32)
        for group in range(3):
            moved = shifted(main, group * room - 2 * owned)
            if group:
                moved = pltpu.roll(moved, 16 - 4 * group, 0)
            here = (lane_half >= group * room) & (lane_half < (group + 1) * room)
            last = jnp.where(here, moved, last)
        return jnp.where(row8 < 4, last[:8], 0.0)

    def pack_kind(kind):
        def pack(x, carry):
            for owner in range(n):
                values = []
                for group in range(3):
                    value = jnp.zeros((8, lanes), f32)
                    for start, a, j, count in pieces(owner, owned, depth):
                        row = pl.multiple_of((a * planes + x) * tail + group * 8, 8)
                        source = lines[kind, pl.ds(row, 8), :]
                        for part in range(2):
                            at = part * owned + start
                            moved = shifted(source, at - (part * depth + j))
                            value = jnp.where((lane8 >= at) & (lane8 < at + count), moved, value)
                    values.append(value)
                send[kind, owner, x] = fold(jnp.concatenate(values[:2], 0), values[2])
            return carry

        lax.fori_loop(0, planes, pack, 0)

    def first_copy(kind, step):
        other = lax.rem(me + step, n)
        return pltpu.make_async_remote_copy(
            src_ref=send.at[kind, other],
            dst_ref=recv.at[kind, me],
            send_sem=send_sem.at[kind, step],
            recv_sem=recv_sem.at[kind, step],
            device_id=(other, mine),
            device_id_type=pl.DeviceIdType.MESH,
        )

    def own_copy(kind):
        return pltpu.make_async_copy(send.at[kind, me], recv.at[kind, me], local_sem.at[kind])

    def start_first(kind):
        def start(step, carry):
            first_copy(kind, step).start()
            return carry

        lax.fori_loop(1, n, start, 0)
        own_copy(kind).start()

    def wait_first(kind):
        def wait(step, carry):
            first_copy(kind, step).wait()
            return carry

        own_copy(kind).wait()
        lax.fori_loop(1, n, wait, 0)

    for chunk in range(chunks):
        load(feat_hbm, feat_ref, feat_sem, chunk).start()
    w_copy = pltpu.make_async_copy(w_hbm, w_ref, w_sem.at[0])
    w_copy.start()
    for chunk in range(chunks):
        load(cot_hbm, cot_ref, cot_sem, chunk).wait()
        lax.fori_loop(chunk * per, (chunk + 1) * per, gradient_lines, 0)
    pack_kind(1)
    pl.semaphore_wait(barrier, n - 1 + peers - 1)
    start_first(1)
    for chunk in range(chunks):
        load(feat_hbm, feat_ref, feat_sem, chunk).wait()
        lax.fori_loop(chunk * per, (chunk + 1) * per, field_lines, 0)
    pack_kind(0)
    start_first(0)

    tall = channels * ROWS
    same = (
        lax.broadcasted_iota(jnp.int32, (tall, tall), 0)
        ^ lax.broadcasted_iota(jnp.int32, (tall, tall), 1)
    ) & (ROWS - 1)
    across = (((1,), (1,)), ((), ()))
    for place, part in enumerate(halves(pw_ref[...])):
        outer = lax.dot_general(expand_ref[...], part, across, preferred_element_type=f32)
        inner = lax.dot_general(
            outer.astype(bf16), expand_ref[...], across, preferred_element_type=f32
        )
        kron_ref[place * tall : (place + 1) * tall, :] = jnp.where(same == 0, inner, 0.0).astype(bf16)

    def mix_cells(x, carry):
        for block in range(0, length, ROWS):
            value = cot_ref[:, x, block : block + ROWS, :].reshape(tall, lanes)
            out = jnp.dot(kron_ref[...], value, preferred_element_type=f32)
            total = out[:tall] + out[tall:]
            point[:, x, block : block + ROWS, :] = total.reshape(channels, ROWS, lanes)
        return carry

    lax.fori_loop(0, planes, mix_cells, 0)

    total_planes = n * planes

    def spec_copy(kind, step):
        other = lax.rem(mine + step, peers)
        return pltpu.make_async_remote_copy(
            src_ref=spec.at[mine, kind],
            dst_ref=spec.at[mine, kind],
            send_sem=spec_send_sem.at[kind, step],
            recv_sem=spec_recv_sem.at[kind, step],
            device_id=(me, other),
            device_id_type=pl.DeviceIdType.MESH,
        )

    def along_x(kind):
        def add_plane(x, carry):
            value = recv[kind, x // planes, lax.rem(x, planes)]
            return tuple(
                carry[t] + plane_ref[t * total_planes + x] * value for t in range(TERMS)
            )

        zero = jnp.zeros((16, lanes), f32)
        sums = lax.fori_loop(0, total_planes, add_plane, (zero,) * TERMS, unroll=4)

        def unpack(t):
            main = jnp.where(lane_half < 2 * owned, sums[t], 0.0)
            return jnp.concatenate([main, unfold(sums[t])], 0)

        for k in range(HALF + 1):
            even = unpack(k)
            if k == 0:
                spec[mine, kind, 0] = even
                continue
            odd = swap(unpack(HALF + k), owned)
            if k < HALF:
                spec[mine, kind, k] = even + odd
            spec[mine, kind, KX - k] = even - odd
        for step in range(1, peers):
            spec_copy(kind, step).start()

    w_copy.wait()
    wait_first(1)
    along_x(1)

    square = channels * channels

    def spread(sample, kind, k):
        high, low = halves(spec[sample, kind, k].T)
        return jnp.dot(
            jnp.concatenate([high, low], 1), spread_ref[kind], preferred_element_type=f32
        )[:, :square]

    for k in range(KX):
        wide = spread(mine, 1, k)
        real, imag = wide[:owned], wide[owned : 2 * owned]
        w_real = w_ref[:, k * 2 * square : (k * 2 + 1) * square].astype(f32)
        w_imag = w_ref[:, (k * 2 + 1) * square : (k * 2 + 2) * square].astype(f32)
        mixed = jnp.concatenate(
            [
                real * w_real + imag * w_imag,
                imag * w_real - real * w_imag,
                jnp.zeros((lanes - 2 * owned, square), f32),
            ],
            0,
        )
        out = None
        for part in halves(mixed):
            term = lax.dot_general(
                collect_ref[...], part, (((1,), (1,)), ((), ())), preferred_element_type=f32
            )
            out = term if out is None else out + term
        adj[k] = out

    def pack_back(value):
        return fold(value[:16], value[16:])

    terms = [pack_back(adj[0])]
    for k in range(1, HALF):
        terms.append(pack_back(adj[k] + adj[KX - k]))
    terms.append(pack_back(adj[HALF]))
    for k in range(1, HALF):
        terms.append(pack_back(swap(adj[KX - k] - adj[k], owned)))
    terms.append(pack_back(swap(adj[HALF], owned)))

    def put_plane(x, carry):
        value = plane_ref[x] * carry[0]
        for t in range(1, TERMS):
            value = value + plane_ref[t * total_planes + x] * carry[t]
        send2[x // planes, lax.rem(x, planes)] = value
        return carry

    lax.fori_loop(0, total_planes, put_plane, tuple(terms), unroll=4)

    def second_copy(step):
        other = lax.rem(me + step, n)
        return pltpu.make_async_remote_copy(
            src_ref=send2.at[other],
            dst_ref=recv2.at[me],
            send_sem=send2_sem.at[step],
            recv_sem=recv2_sem.at[step],
            device_id=(other, mine),
            device_id_type=pl.DeviceIdType.MESH,
        )

    def start_second(step, carry):
        second_copy(step).start()
        return carry

    lax.fori_loop(1, n, start_second, 0)
    local2 = pltpu.make_async_copy(send2.at[me], recv2.at[me], local_sem.at[2])
    local2.start()

    wait_first(0)
    along_x(0)
    for kind in range(2):
        for step in range(1, peers):
            spec_copy(kind, step).wait()

    for k in range(KX):
        out_real = out_imag = None
        for sample in range(peers):
            wide, g_wide = spread(sample, 0, k), spread(sample, 1, k)
            s_real, s_imag = wide[:owned], wide[owned : 2 * owned]
            g_real, g_imag = g_wide[:owned], g_wide[owned : 2 * owned]
            t_real = s_real * g_real + s_imag * g_imag
            t_imag = s_real * g_imag - s_imag * g_real
            out_real = t_real if out_real is None else out_real + t_real
            out_imag = t_imag if out_imag is None else out_imag + t_imag
        gw_ref[:, k * 2 * square : (k * 2 + 1) * square] = out_real
        gw_ref[:, (k * 2 + 1) * square : (k * 2 + 2) * square] = out_imag

    gw_copy = pltpu.make_async_copy(gw_ref, gw_hbm, gw_sem.at[0])
    gw_copy.start()
    local2.wait()

    def wait_second(step, carry):
        second_copy(step).wait()
        return carry

    lax.fori_loop(1, n, wait_second, 0)

    def unpack_back(x, carry):
        wholes = {}
        for owner in range(n):
            main = recv2[owner, x]
            wholes[owner] = (main[:8], main[8:16], unfold(main))
            for a in range(KY):
                first = a * depth // owned
                final = ((a + 1) * depth - 1) // owned
                if final != owner:
                    continue
                for group in range(3):
                    value = jnp.zeros((8, lanes), f32)
                    for source in range(first, final + 1):
                        for start, row, j, count in pieces(source, owned, depth):
                            if row != a:
                                continue
                            for part in range(2):
                                at = part * depth + j
                                moved = shifted(wholes[source][group], at - (part * owned + start))
                                value = jnp.where(
                                    (lane8 >= at) & (lane8 < at + count), moved, value
                                )
                    place = pl.multiple_of((a * planes + x) * tail + group * 8, 8)
                    back[pl.ds(place, 8), :] = value
        for a in range(KY, PAD):
            for group in range(3):
                place = pl.multiple_of((a * planes + x) * tail + group * 8, 8)
                back[pl.ds(place, 8), :] = jnp.zeros((8, lanes), f32)
        return carry

    lax.fori_loop(0, planes, unpack_back, 0)

    def gf_copy(c):
        return pltpu.make_async_copy(gf_ref.at[c], gf_hbm.at[c], gf_sem.at[c])

    def finish(c, carry):
        for first in range(0, planes, pair):
            blocks = []
            for k in range(pair):
                value = back[pl.ds((first + k) * tail + c, PAD, stride=planes * tail), :]
                turned = -sign * pltpu.roll(value, depth, 1)
                blocks.append(jnp.concatenate([value, turned], 0))
            high, low = halves(jnp.concatenate(blocks, 1))
            out = jnp.dot(
                bwd_ref[...], jnp.concatenate([high, low, high], 0), preferred_element_type=f32
            )
            for k in range(pair):
                gf_ref[c, first + k] = (
                    point[c, first + k] + out[:, k * lanes : (k + 1) * lanes]
                ).astype(bf16)
        gf_copy(c).start()
        return carry

    lax.fori_loop(0, channels, finish, 0)

    def settle(c, carry):
        gf_copy(c).wait()
        return carry

    lax.fori_loop(0, channels, settle, 0)
    gw_copy.wait()


def shards(features, cotangent, spectral_weight, pointwise_weight):
    _, channels, planes, length, lanes = features.shape
    owned = spectral_weight.shape[0]
    n = lax.axis_size("slab")
    peers = lax.axis_size("batch")
    tail = 24
    square = channels * channels
    width = -(-square // 128) * 128
    chunks = math.gcd(channels, 5)
    vmem = pl.BlockSpec(memory_space=pltpu.VMEM)
    grad_features, grad_spectral = pl.pallas_call(
        functools.partial(kernel, n, peers),
        out_shape=(
            jax.ShapeDtypeStruct(features.shape[1:], bf16),
            jax.ShapeDtypeStruct(spectral_weight.shape, f32),
        ),
        in_specs=[pl.BlockSpec(memory_space=pl.ANY)] * 3 + [vmem] * 6 + [pl.BlockSpec(memory_space=pltpu.SMEM)],
        out_specs=(pl.BlockSpec(memory_space=pl.ANY),) * 2,
        scratch_shapes=[
            pltpu.VMEM(features.shape[1:], f32),
            pltpu.VMEM(cotangent.shape[1:], bf16),
            pltpu.VMEM(spectral_weight.shape, bf16),
            pltpu.VMEM(features.shape[1:], bf16),
            pltpu.VMEM(spectral_weight.shape, f32),
            pltpu.VMEM((2, PAD * planes * tail, lanes), f32),
            pltpu.VMEM((2, n, planes, 16, lanes), f32),
            pltpu.VMEM((2, n, planes, 16, lanes), f32),
            pltpu.VMEM((peers, 2, KX, tail, lanes), f32),
            pltpu.VMEM((KX, 24, lanes), f32),
            pltpu.VMEM((n, planes, 16, lanes), f32),
            pltpu.VMEM((n, planes, 16, lanes), f32),
            pltpu.VMEM((PAD * planes * 24, lanes), f32),
            pltpu.VMEM((channels, planes, length, lanes), f32),
            pltpu.VMEM((2 * channels * ROWS, channels * ROWS), bf16),
            pltpu.SemaphoreType.DMA((2, n)),
            pltpu.SemaphoreType.DMA((2, n)),
            pltpu.SemaphoreType.DMA((n,)),
            pltpu.SemaphoreType.DMA((n,)),
            pltpu.SemaphoreType.DMA((2, peers)),
            pltpu.SemaphoreType.DMA((2, peers)),
            pltpu.SemaphoreType.DMA((3,)),
            pltpu.SemaphoreType.DMA((chunks,)),
            pltpu.SemaphoreType.DMA((chunks,)),
            pltpu.SemaphoreType.DMA((1,)),
            pltpu.SemaphoreType.DMA((channels,)),
            pltpu.SemaphoreType.DMA((1,)),
        ],
        compiler_params=pltpu.CompilerParams(
            collective_id=0, has_side_effects=True, vmem_limit_bytes=58 * 1024 * 1024
        ),
    )(
        features[0],
        cotangent[0],
        spectral_weight,
        pointwise_weight,
        jnp.asarray(np.repeat(np.eye(channels), ROWS, 0).astype(jnp.bfloat16)),
        jnp.asarray(forward_table(length)),
        jnp.asarray(backward_table(length)),
        jnp.asarray(spread_tables(channels, tail, width)),
        jnp.asarray(collect_table(channels, 24, square)),
        jnp.asarray(plane_terms(planes * n)),
    )
    return grad_features[None], grad_spectral


def solution(mesh):
    placed = (
        P("batch", None, "slab", None, None),
        P("batch", None, "slab", None, None),
        P("slab", None),
        P(),
    )
    return jax.shard_map(
        shards,
        mesh=mesh,
        in_specs=placed,
        out_specs=(P("batch", None, "slab", None, None), P("slab", None)),
        check_vma=False,
    )
```

```python
import functools
import math

import jax
import jax.numpy as jnp
import numpy as np
from jax import lax
from jax.experimental import pallas as pl
from jax.experimental.pallas import tpu as pltpu
from jax.sharding import PartitionSpec as P

KX = 12
KY = 12
PAD = 16
HALF = KX // 2
TERMS = KX + 1
ROWS = 16

f32 = jnp.float32
bf16 = jnp.bfloat16


def angles(count, length):
    steps = np.arange(count)
    signed = np.where(steps < count // 2, steps, steps - count)
    turns = np.mod(signed[:, None] * np.arange(length)[None, :], length)
    return turns * (2.0 * math.pi / length)


def halves(value):
    high = value.astype(bf16)
    return high, (value - high.astype(f32)).astype(bf16)


def np_halves(value):
    value = np.asarray(value, np.float32)
    high = value.astype(jnp.bfloat16)
    return high, (value - high.astype(np.float32)).astype(jnp.bfloat16)


def padded(table, rows):
    return np.concatenate([table, np.zeros((rows - table.shape[0], table.shape[1]))], 0)


def forward_table(length):
    angle = angles(KY, length)
    both = np.concatenate([padded(np.cos(angle), PAD), padded(np.sin(angle), PAD)], 0)
    high, low = np_halves(both)
    top = np.concatenate([high, high], 1)
    bottom = np.concatenate([low, np.zeros_like(low)], 1)
    return np.concatenate([top, bottom], 0)


def backward_table(length):
    angle = angles(KY, length)
    both = np.concatenate([padded(np.cos(angle), PAD), padded(np.sin(angle), PAD)], 0).T
    high, low = np_halves(both)
    return np.concatenate([high, high, low], 1)


def plane_terms(length):
    turns = np.mod(np.arange(HALF + 1)[:, None] * np.arange(length)[None, :], length)
    angle = turns * (2.0 * math.pi / length)
    return np.concatenate([np.cos(angle), np.sin(angle)[1:]], 0).astype(np.float32).reshape(-1)


def spread_tables(channels, rows, width):
    tables = np.zeros((2, rows, width), np.float32)
    for c in range(channels):
        for o in range(channels):
            tables[0, c, c * channels + o] = 1.0
            tables[1, o, c * channels + o] = 1.0
    return np.concatenate([tables, tables], 1).astype(jnp.bfloat16)


def collect_table(channels, rows, width):
    table = np.zeros((rows, width), np.float32)
    for c in range(channels):
        table[c, c * channels : (c + 1) * channels] = 1.0
    return table.astype(jnp.bfloat16)


def swap(value, owned):
    lane = lax.broadcasted_iota(jnp.int32, value.shape, 1)
    up = pltpu.roll(value, owned, 1)
    down = pltpu.roll(value, 128 - owned, 1)
    return jnp.where(lane < owned, down, jnp.where(lane < 2 * owned, -up, 0.0))


def pieces(owner, owned, depth):
    out = []
    mode = owner * owned
    while mode < (owner + 1) * owned:
        a, j = divmod(mode, depth)
        count = min(depth - j, (owner + 1) * owned - mode)
        out.append((mode - owner * owned, a, j, count))
        mode += count
    return out


def shifted(value, amount):
    amount %= 128
    return value if amount == 0 else pltpu.roll(value, amount, 1)


def kernel(
    n,
    peers,
    feat_hbm,
    cot_hbm,
    w_hbm,
    pw_ref,
    expand_ref,
    fwd_ref,
    bwd_ref,
    spread_ref,
    collect_ref,
    plane_ref,
    gf_hbm,
    gw_hbm,
    feat_ref,
    cot_ref,
    w_ref,
    gf_ref,
    gw_ref,
    lines,
    send,
    recv,
    spec,
    adj,
    send2,
    recv2,
    back,
    point,
    kron_ref,
    send_sem,
    recv_sem,
    send2_sem,
    recv2_sem,
    spec_send_sem,
    spec_recv_sem,
    local_sem,
    cot_sem,
    feat_sem,
    w_sem,
    gf_sem,
    gw_sem,
):
    channels, planes, length, lanes = feat_ref.shape
    depth = lanes // 2
    owned = w_ref.shape[0]
    tail = 24
    me = lax.axis_index("slab")
    mine = lax.axis_index("batch")
    scale = 1.0 / (planes * n * length)
    pair = 2

    chunks = cot_sem.shape[0]
    per = channels // chunks

    def load(source, target, sem, chunk):
        at = pl.ds(chunk * per, per)
        return pltpu.make_async_copy(source.at[at], target.at[at], sem.at[chunk])

    for chunk in range(chunks):
        load(cot_hbm, cot_ref, cot_sem, chunk).start()
    barrier = pltpu.get_barrier_semaphore()

    def greet(step, carry):
        pl.semaphore_signal(
            barrier, inc=1, device_id=(lax.rem(me + step, n), mine), device_id_type=pl.DeviceIdType.MESH
        )
        return carry

    lax.fori_loop(1, n, greet, 0)

    def greet_batch(step, carry):
        pl.semaphore_signal(
            barrier, inc=1, device_id=(me, lax.rem(mine + step, peers)), device_id_type=pl.DeviceIdType.MESH
        )
        return carry

    lax.fori_loop(1, peers, greet_batch, 0)

    lane16 = lax.broadcasted_iota(jnp.int32, (PAD, lanes), 1)
    sign = jnp.where(lane16 < depth, 1.0, -1.0).astype(f32)

    def store_lines(out, kind, first, c):
        total = out[: 2 * PAD] + out[2 * PAD :]
        for k in range(pair):
            part = total[:, k * lanes : (k + 1) * lanes]
            value = part[:PAD] + sign * pltpu.roll(part[PAD:], depth, 1)
            if kind:
                value = value * scale
            lines[kind, pl.ds((first + k) * tail + c, PAD, stride=planes * tail), :] = value

    def field_lines(c, carry):
        for first in range(0, planes, pair):
            block = jnp.concatenate([feat_ref[c, first + k] for k in range(pair)], 1)
            high, low = halves(block)
            out = jnp.dot(
                fwd_ref[...], jnp.concatenate([high, low], 0), preferred_element_type=f32
            )
            store_lines(out, 0, first, c)
        return carry

    def gradient_lines(c, carry):
        for first in range(0, planes, pair):
            block = jnp.concatenate([cot_ref[c, first + k] for k in range(pair)], 1)
            out = jnp.dot(fwd_ref[:, :length], block, preferred_element_type=f32)
            store_lines(out, 1, first, c)
        return carry

    lane8 = lax.broadcasted_iota(jnp.int32, (8, lanes), 1)
    row8 = lax.broadcasted_iota(jnp.int32, (8, lanes), 0)
    lane_half = lax.broadcasted_iota(jnp.int32, (16, lanes), 1)
    row_half = lax.broadcasted_iota(jnp.int32, (16, lanes), 0)
    room = lanes - 2 * owned

    def fold(main, last):
        last = jnp.concatenate([last, jnp.zeros((8, lanes), f32)], 0)
        for group in range(3):
            moved = shifted(last, 2 * owned - group * room)
            if group:
                moved = pltpu.roll(moved, 4 * group, 0)
            here = (lane_half >= 2 * owned) & (row_half >= 4 * group) & (row_half < 4 * group + 4)
            main = jnp.where(here, moved, main)
        return main

    def unfold(main):
        last = jnp.zeros((16, lanes), f32)
        for group in range(3):
            moved = shifted(main, group * room - 2 * owned)
            if group:
                moved = pltpu.roll(moved, 16 - 4 * group, 0)
            here = (lane_half >= group * room) & (lane_half < (group + 1) * room)
            last = jnp.where(here, moved, last)
        return jnp.where(row8 < 4, last[:8], 0.0)

    def pack_kind(kind):
        def pack(x, carry):
            for owner in range(n):
                values = []
                for group in range(3):
                    value = jnp.zeros((8, lanes), f32)
                    for start, a, j, count in pieces(owner, owned, depth):
                        row = pl.multiple_of((a * planes + x) * tail + group * 8, 8)
                        source = lines[kind, pl.ds(row, 8), :]
                        for part in range(2):
                            at = part * owned + start
                            moved = shifted(source, at - (part * depth + j))
                            value = jnp.where((lane8 >= at) & (lane8 < at + count), moved, value)
                    values.append(value)
                send[kind, owner, x] = fold(jnp.concatenate(values[:2], 0), values[2])
            return carry

        lax.fori_loop(0, planes, pack, 0)

    def first_copy(kind, step):
        other = lax.rem(me + step, n)
        return pltpu.make_async_remote_copy(
            src_ref=send.at[kind, other],
            dst_ref=recv.at[kind, me],
            send_sem=send_sem.at[kind, step],
            recv_sem=recv_sem.at[kind, step],
            device_id=(other, mine),
            device_id_type=pl.DeviceIdType.MESH,
        )

    def own_copy(kind):
        return pltpu.make_async_copy(send.at[kind, me], recv.at[kind, me], local_sem.at[kind])

    def start_first(kind):
        def start(step, carry):
            first_copy(kind, step).start()
            return carry

        lax.fori_loop(1, n, start, 0)
        own_copy(kind).start()

    for chunk in range(chunks):
        load(feat_hbm, feat_ref, feat_sem, chunk).start()
    w_copy = pltpu.make_async_copy(w_hbm, w_ref, w_sem.at[0])
    w_copy.start()
    for chunk in range(chunks):
        load(cot_hbm, cot_ref, cot_sem, chunk).wait()
        lax.fori_loop(chunk * per, (chunk + 1) * per, gradient_lines, 0)
    pack_kind(1)
    pl.semaphore_wait(barrier, n - 1 + peers - 1)
    start_first(1)
    for chunk in range(chunks):
        load(feat_hbm, feat_ref, feat_sem, chunk).wait()
        lax.fori_loop(chunk * per, (chunk + 1) * per, field_lines, 0)
    pack_kind(0)
    start_first(0)

    tall = channels * ROWS
    same = (
        lax.broadcasted_iota(jnp.int32, (tall, tall), 0)
        ^ lax.broadcasted_iota(jnp.int32, (tall, tall), 1)
    ) & (ROWS - 1)
    across = (((1,), (1,)), ((), ()))
    for place, part in enumerate(halves(pw_ref[...])):
        outer = lax.dot_general(expand_ref[...], part, across, preferred_element_type=f32)
        inner = lax.dot_general(
            outer.astype(bf16), expand_ref[...], across, preferred_element_type=f32
        )
        kron_ref[place * tall : (place + 1) * tall, :] = jnp.where(same == 0, inner, 0.0).astype(bf16)

    def mix_cells(x, carry):
        for block in range(0, length, ROWS):
            value = cot_ref[:, x, block : block + ROWS, :].reshape(tall, lanes)
            out = jnp.dot(kron_ref[...], value, preferred_element_type=f32)
            total = out[:tall] + out[tall:]
            point[:, x, block : block + ROWS, :] = total.reshape(channels, ROWS, lanes)
        return carry

    lax.fori_loop(0, planes, mix_cells, 0)

    total_planes = n * planes

    def spec_copy(kind, step):
        other = lax.rem(mine + step, peers)
        return pltpu.make_async_remote_copy(
            src_ref=spec.at[mine, kind],
            dst_ref=spec.at[mine, kind],
            send_sem=spec_send_sem.at[kind, step],
            recv_sem=spec_recv_sem.at[kind, step],
            device_id=(me, other),
            device_id_type=pl.DeviceIdType.MESH,
        )

    def along_x(kind):
        def add_source(source, carry):
            for plane in range(planes):
                value = recv[kind, source, plane]
                at = source * planes + plane
                carry = tuple(
                    carry[t] + plane_ref[t * total_planes + at] * value for t in range(TERMS)
                )
            return carry

        def add_step(step, carry):
            first_copy(kind, step).wait()
            return add_source(lax.rem(me - step + n, n), carry)

        own_copy(kind).wait()
        zero = jnp.zeros((16, lanes), f32)
        sums = lax.fori_loop(1, n, add_step, add_source(me, (zero,) * TERMS))

        def unpack(t):
            main = jnp.where(lane_half < 2 * owned, sums[t], 0.0)
            return jnp.concatenate([main, unfold(sums[t])], 0)

        for k in range(HALF + 1):
            even = unpack(k)
            if k == 0:
                spec[mine, kind, 0] = even
                continue
            odd = swap(unpack(HALF + k), owned)
            if k < HALF:
                spec[mine, kind, k] = even + odd
            spec[mine, kind, KX - k] = even - odd
        for step in range(1, peers):
            spec_copy(kind, step).start()

    w_copy.wait()
    along_x(1)

    square = channels * channels

    def spread(sample, kind, k):
        high, low = halves(spec[sample, kind, k].T)
        return jnp.dot(
            jnp.concatenate([high, low], 1), spread_ref[kind], preferred_element_type=f32
        )[:, :square]

    for k in range(KX):
        wide = spread(mine, 1, k)
        real, imag = wide[:owned], wide[owned : 2 * owned]
        w_real = w_ref[:, k * 2 * square : (k * 2 + 1) * square].astype(f32)
        w_imag = w_ref[:, (k * 2 + 1) * square : (k * 2 + 2) * square].astype(f32)
        mixed = jnp.concatenate(
            [
                real * w_real + imag * w_imag,
                imag * w_real - real * w_imag,
                jnp.zeros((lanes - 2 * owned, square), f32),
            ],
            0,
        )
        out = None
        for part in halves(mixed):
            term = lax.dot_general(
                collect_ref[...], part, (((1,), (1,)), ((), ())), preferred_element_type=f32
            )
            out = term if out is None else out + term
        adj[k] = out

    def pack_back(value):
        return fold(value[:16], value[16:])

    terms = [pack_back(adj[0])]
    for k in range(1, HALF):
        terms.append(pack_back(adj[k] + adj[KX - k]))
    terms.append(pack_back(adj[HALF]))
    for k in range(1, HALF):
        terms.append(pack_back(swap(adj[KX - k] - adj[k], owned)))
    terms.append(pack_back(swap(adj[HALF], owned)))

    def put_plane(x, carry):
        value = plane_ref[x] * carry[0]
        for t in range(1, TERMS):
            value = value + plane_ref[t * total_planes + x] * carry[t]
        send2[x // planes, lax.rem(x, planes)] = value
        return carry

    lax.fori_loop(0, total_planes, put_plane, tuple(terms), unroll=4)

    def second_copy(step):
        other = lax.rem(me + step, n)
        return pltpu.make_async_remote_copy(
            src_ref=send2.at[other],
            dst_ref=recv2.at[me],
            send_sem=send2_sem.at[step],
            recv_sem=recv2_sem.at[step],
            device_id=(other, mine),
            device_id_type=pl.DeviceIdType.MESH,
        )

    def start_second(step, carry):
        second_copy(step).start()
        return carry

    lax.fori_loop(1, n, start_second, 0)
    local2 = pltpu.make_async_copy(send2.at[me], recv2.at[me], local_sem.at[2])
    local2.start()

    along_x(0)
    for kind in range(2):
        for step in range(1, peers):
            spec_copy(kind, step).wait()

    for k in range(KX):
        out_real = out_imag = None
        for sample in range(peers):
            wide, g_wide = spread(sample, 0, k), spread(sample, 1, k)
            s_real, s_imag = wide[:owned], wide[owned : 2 * owned]
            g_real, g_imag = g_wide[:owned], g_wide[owned : 2 * owned]
            t_real = s_real * g_real + s_imag * g_imag
            t_imag = s_real * g_imag - s_imag * g_real
            out_real = t_real if out_real is None else out_real + t_real
            out_imag = t_imag if out_imag is None else out_imag + t_imag
        gw_ref[:, k * 2 * square : (k * 2 + 1) * square] = out_real
        gw_ref[:, (k * 2 + 1) * square : (k * 2 + 2) * square] = out_imag

    gw_copy = pltpu.make_async_copy(gw_ref, gw_hbm, gw_sem.at[0])
    gw_copy.start()
    local2.wait()

    def wait_second(step, carry):
        second_copy(step).wait()
        return carry

    lax.fori_loop(1, n, wait_second, 0)

    def unpack_back(x, carry):
        wholes = {}
        for owner in range(n):
            main = recv2[owner, x]
            wholes[owner] = (main[:8], main[8:16], unfold(main))
            for a in range(KY):
                first = a * depth // owned
                final = ((a + 1) * depth - 1) // owned
                if final != owner:
                    continue
                for group in range(3):
                    value = jnp.zeros((8, lanes), f32)
                    for source in range(first, final + 1):
                        for start, row, j, count in pieces(source, owned, depth):
                            if row != a:
                                continue
                            for part in range(2):
                                at = part * depth + j
                                moved = shifted(wholes[source][group], at - (part * owned + start))
                                value = jnp.where(
                                    (lane8 >= at) & (lane8 < at + count), moved, value
                                )
                    place = pl.multiple_of((a * planes + x) * tail + group * 8, 8)
                    back[pl.ds(place, 8), :] = value
        for a in range(KY, PAD):
            for group in range(3):
                place = pl.multiple_of((a * planes + x) * tail + group * 8, 8)
                back[pl.ds(place, 8), :] = jnp.zeros((8, lanes), f32)
        return carry

    lax.fori_loop(0, planes, unpack_back, 0)

    def gf_copy(c):
        return pltpu.make_async_copy(gf_ref.at[c], gf_hbm.at[c], gf_sem.at[c])

    def finish(c, carry):
        for first in range(0, planes, pair):
            blocks = []
            for k in range(pair):
                value = back[pl.ds((first + k) * tail + c, PAD, stride=planes * tail), :]
                turned = -sign * pltpu.roll(value, depth, 1)
                blocks.append(jnp.concatenate([value, turned], 0))
            high, low = halves(jnp.concatenate(blocks, 1))
            out = jnp.dot(
                bwd_ref[...], jnp.concatenate([high, low, high], 0), preferred_element_type=f32
            )
            for k in range(pair):
                gf_ref[c, first + k] = (
                    point[c, first + k] + out[:, k * lanes : (k + 1) * lanes]
                ).astype(bf16)
        gf_copy(c).start()
        return carry

    lax.fori_loop(0, channels, finish, 0)

    def settle(c, carry):
        gf_copy(c).wait()
        return carry

    lax.fori_loop(0, channels, settle, 0)
    gw_copy.wait()


def shards(features, cotangent, spectral_weight, pointwise_weight):
    _, channels, planes, length, lanes = features.shape
    owned = spectral_weight.shape[0]
    n = lax.axis_size("slab")
    peers = lax.axis_size("batch")
    tail = 24
    square = channels * channels
    width = -(-square // 128) * 128
    chunks = math.gcd(channels, 5)
    vmem = pl.BlockSpec(memory_space=pltpu.VMEM)
    grad_features, grad_spectral = pl.pallas_call(
        functools.partial(kernel, n, peers),
        out_shape=(
            jax.ShapeDtypeStruct(features.shape[1:], bf16),
            jax.ShapeDtypeStruct(spectral_weight.shape, f32),
        ),
        in_specs=[pl.BlockSpec(memory_space=pl.ANY)] * 3 + [vmem] * 6 + [pl.BlockSpec(memory_space=pltpu.SMEM)],
        out_specs=(pl.BlockSpec(memory_space=pl.ANY),) * 2,
        scratch_shapes=[
            pltpu.VMEM(features.shape[1:], f32),
            pltpu.VMEM(cotangent.shape[1:], bf16),
            pltpu.VMEM(spectral_weight.shape, bf16),
            pltpu.VMEM(features.shape[1:], bf16),
            pltpu.VMEM(spectral_weight.shape, f32),
            pltpu.VMEM((2, PAD * planes * tail, lanes), f32),
            pltpu.VMEM((2, n, planes, 16, lanes), f32),
            pltpu.VMEM((2, n, planes, 16, lanes), f32),
            pltpu.VMEM((peers, 2, KX, tail, lanes), f32),
            pltpu.VMEM((KX, 24, lanes), f32),
            pltpu.VMEM((n, planes, 16, lanes), f32),
            pltpu.VMEM((n, planes, 16, lanes), f32),
            pltpu.VMEM((PAD * planes * 24, lanes), f32),
            pltpu.VMEM((channels, planes, length, lanes), f32),
            pltpu.VMEM((2 * channels * ROWS, channels * ROWS), bf16),
            pltpu.SemaphoreType.DMA((2, n)),
            pltpu.SemaphoreType.DMA((2, n)),
            pltpu.SemaphoreType.DMA((n,)),
            pltpu.SemaphoreType.DMA((n,)),
            pltpu.SemaphoreType.DMA((2, peers)),
            pltpu.SemaphoreType.DMA((2, peers)),
            pltpu.SemaphoreType.DMA((3,)),
            pltpu.SemaphoreType.DMA((chunks,)),
            pltpu.SemaphoreType.DMA((chunks,)),
            pltpu.SemaphoreType.DMA((1,)),
            pltpu.SemaphoreType.DMA((channels,)),
            pltpu.SemaphoreType.DMA((1,)),
        ],
        compiler_params=pltpu.CompilerParams(
            collective_id=0, has_side_effects=True, vmem_limit_bytes=58 * 1024 * 1024
        ),
    )(
        features[0],
        cotangent[0],
        spectral_weight,
        pointwise_weight,
        jnp.asarray(np.repeat(np.eye(channels), ROWS, 0).astype(jnp.bfloat16)),
        jnp.asarray(forward_table(length)),
        jnp.asarray(backward_table(length)),
        jnp.asarray(spread_tables(channels, tail, width)),
        jnp.asarray(collect_table(channels, 24, square)),
        jnp.asarray(plane_terms(planes * n)),
    )
    return grad_features[None], grad_spectral


def solution(mesh):
    placed = (
        P("batch", None, "slab", None, None),
        P("batch", None, "slab", None, None),
        P("slab", None),
        P(),
    )
    return jax.shard_map(
        shards,
        mesh=mesh,
        in_specs=placed,
        out_specs=(P("batch", None, "slab", None, None), P("slab", None)),
        check_vma=False,
    )
```
